256 devices in a mesh: layer: 4 (over x), row: 8 (over z_hi, core), col: 8 (over y, z_lo).
Axes of the slice: x: 4, y: 4, z: 8 (z_hi: 4, z_lo: 2; z = z_hi * 2 + z_lo), core: 2. Of those that a mesh axis runs over, the one named last changes fastest.
Arguments:
- even_left: bfloat16 [2, 4, 32, 32, 256, 128], P(None, 'layer', 'row', 'col'), may hold values from -0.09375 to 0.09375
- even_right: bfloat16 [2, 4, 32, 32, 256, 128], P(None, 'layer', 'row', 'col'), may hold values from -0.25 to 0.25
- odd_left: bfloat16 [2, 4, 32, 32, 256, 128], P(None, 'layer', 'col', 'row'), may hold values from -0.09375 to 0.09375
- odd_right: bfloat16 [2, 4, 32, 32, 256, 128], P(None, 'layer', 'col', 'row'), may hold values from -0.25 to 0.25
- even_ranks: int32 [2, 4, 32, 32], P(None, 'layer', 'row', 'col'), may hold values from 16 to 64, as said below
- odd_ranks: int32 [2, 4, 32, 32], P(None, 'layer', 'col', 'row'), may hold values from 16 to 64, as said below
- even_sources: float32 [2, 4, 2, 8192, 128], P(None, 'layer', None, ('row', 'col')), may hold values from -6 to 6
- odd_sources: float32 [2, 4, 2, 8192, 128], P(None, 'layer', None, ('col', 'row')), may hold values from -6 to 6
Outputs:
- even_traces: float32 [4, 2, 8192, 128], P('layer', None, ('row', 'col'))
- odd_traces: float32 [4, 2, 8192, 128], P('layer', None, ('col', 'row'))
The draws below stay inside these ranges and needn't reach their ends.
Inputs may be any that keep to these rules, and one draw needn't show every extreme that they name: `even_ranks`: every direction and pair has a tile of rank 64 and a tile of rank a quarter of 64. `odd_ranks`: every direction and pair has a tile of rank 64 and a tile of rank a quarter of 64.
All inputs are finite; a program needn't handle non-finite values.
Results may differ from the reference program's by a relative error of at most 0.008.
Values may be sent and summed in bfloat16 or wider, within the bound.
No kernel may reach another device: no remote copies, remote signals or barrier semaphores. Data moves between devices by JAX's collectives and lax.ppermute only.
A program may use at most 128 MiB of HBM per device.

```python
import jax
import jax.numpy as jnp
from jax import lax

NT = 8192
TILE = 256
RMAX = 64
BATCH = 64
NB = 2
TILES = 32
PAIRS = 4
LAYERS = 8


def rank_table(seed_key):
    total = TILES * TILES
    drawn = jax.random.randint(jax.random.fold_in(seed_key, 11), (2, PAIRS, total), RMAX // 4, RMAX + 1)
    top_spot = jax.random.randint(jax.random.fold_in(seed_key, 12), (2, PAIRS, 1), 0, total)
    offset = jax.random.randint(jax.random.fold_in(seed_key, 13), (2, PAIRS, 1), 0, total - 1)
    low_spot = (top_spot + 1 + offset) % total
    places = lax.iota(jnp.int32, total)[None, None, :]
    rank_grid = jnp.where(places == top_spot, RMAX, drawn)
    rank_grid = jnp.where(places == low_spot, RMAX // 4, rank_grid)
    return rank_grid.reshape(2, PAIRS, TILES, TILES).astype(jnp.int32)


def draw_even_ranks(key, part):
    return rank_table(jax.random.fold_in(key, 1))


def draw_odd_ranks(key, part):
    return rank_table(jax.random.fold_in(key, 2))


def shard_levels(key, shape, shards, low, high):
    level, own = 1.0, jax.random.fold_in(key, 6)
    for position, blocks in shards:
        steps = jnp.exp(jax.random.uniform(jax.random.fold_in(own, position), (blocks,), jnp.float32, low / len(shards), high / len(shards)))
        level = level * jnp.repeat(steps, shape[position] // blocks).reshape([-1 if axis == position else 1 for axis in range(len(shape))])
    return level


def centred(key, extent, scale, reach, cuts=(), dtype=jnp.bfloat16):
    array = jax.random.normal(key, extent, jnp.float32) * scale
    if len(cuts) > 0:
        array = shard_levels(key, extent, cuts, -0.22, 0.18) * array
    return jnp.clip(array, min=-reach, max=reach).astype(dtype)


def setup_inputs(seed: int = 0) -> dict:
    arg_keys = jax.random.split(jax.random.key(seed), 9)
    even_left = centred(arg_keys[0], (2, PAIRS, TILES, TILES, TILE, 2 * RMAX), (2 * RMAX * TILES) ** -0.5, 0.09375, ((1, 4), (2, 8), (3, 8)))
    even_right = centred(arg_keys[1], (2, PAIRS, TILES, TILES, TILE, 2 * RMAX), (2 * TILE) ** -0.5, 0.25, ((1, 4), (2, 8), (3, 8)))
    odd_left = centred(arg_keys[2], (2, PAIRS, TILES, TILES, TILE, 2 * RMAX), (2 * RMAX * TILES) ** -0.5, 0.09375, ((1, 4), (2, 8), (3, 8)))
    odd_right = centred(arg_keys[3], (2, PAIRS, TILES, TILES, TILE, 2 * RMAX), (2 * TILE) ** -0.5, 0.25, ((1, 4), (2, 8), (3, 8)))
    even_ranks = draw_even_ranks(jax.random.fold_in(arg_keys[8], 71), 0)
    odd_ranks = draw_odd_ranks(jax.random.fold_in(arg_keys[8], 71), 0)
    even_sources = centred(arg_keys[6], (2, PAIRS, NB, NT, 2 * BATCH), 1.0, 6.0, ((1, 4), (3, 64)), jnp.float32)
    odd_sources = centred(arg_keys[7], (2, PAIRS, NB, NT, 2 * BATCH), 1.0, 6.0, ((1, 4), (3, 64)), jnp.float32)
    return dict(even_left=even_left, even_right=even_right, odd_left=odd_left, odd_right=odd_right, even_ranks=even_ranks, odd_ranks=odd_ranks, even_sources=even_sources, odd_sources=odd_sources)


def tile_product(gathered, left_factor, right_factor, tile_ranks):
    batch_count = gathered.shape[0]
    tile_rows, tile_cols, tile_size, twice_rank = right_factor.shape
    half_rank = twice_rank // 2
    width = gathered.shape[2]
    half_cols = width // 2
    traces = gathered.reshape(batch_count, tile_cols, tile_size, width).astype(jnp.float32)
    products = jnp.einsum('acnr,kcnb->kacrb', right_factor.astype(jnp.float32), traces, preferred_element_type=jnp.float32)
    real_part = products[:, :, :, :half_rank, :half_cols] - products[:, :, :, half_rank:, half_cols:]
    imag_part = products[:, :, :, :half_rank, half_cols:] + products[:, :, :, half_rank:, :half_cols]
    rank_mask = (lax.iota(jnp.int32, half_rank)[None, None, :] < tile_ranks[:, :, None]).astype(jnp.float32)
    rank_mask = rank_mask[None, :, :, :, None]
    real_part = real_part * rank_mask
    imag_part = imag_part * rank_mask
    stacked = jnp.concatenate([jnp.concatenate([real_part, imag_part], axis=4), jnp.concatenate([-imag_part, real_part], axis=4)], axis=3).astype(jnp.bfloat16)
    result = jnp.einsum('acmr,kacrb->kamb', left_factor.astype(jnp.float32), stacked.astype(jnp.float32), preferred_element_type=jnp.float32)
    return result.reshape(batch_count, tile_rows * tile_size, width)


def reference(even_left, even_right, odd_left, odd_right, even_ranks, odd_ranks, even_sources, odd_sources):
    def pick(layer_index, direction):
        pair_index = layer_index // 2
        if layer_index % 2 == 0:
            return even_left[direction, pair_index], even_right[direction, pair_index], even_ranks[direction, pair_index], even_sources[direction, pair_index]
        return odd_left[direction, pair_index], odd_right[direction, pair_index], odd_ranks[direction, pair_index], odd_sources[direction, pair_index]

    down_traces = []
    current = jnp.zeros((NB, NT, 2 * BATCH), jnp.float32)
    for layer_index in range(LAYERS):
        left_factor, right_factor, tile_ranks, sources = pick(layer_index, 0)
        current = tile_product(current.astype(jnp.bfloat16), left_factor, right_factor, tile_ranks) + sources
        down_traces.append(current)
    up_traces = [None] * LAYERS
    current = jnp.zeros((NB, NT, 2 * BATCH), jnp.float32)
    for layer_index in reversed(range(LAYERS)):
        left_factor, right_factor, tile_ranks, sources = pick(layer_index, 1)
        current = tile_product(current.astype(jnp.bfloat16), left_factor, right_factor, tile_ranks) + sources
        up_traces[layer_index] = current
    even_traces = jnp.stack([down_traces[2 * pair_index] + up_traces[2 * pair_index] for pair_index in range(PAIRS)])
    odd_traces = jnp.stack([down_traces[2 * pair_index + 1] + up_traces[2 * pair_index + 1] for pair_index in range(PAIRS)])
    return even_traces, odd_traces
```

```python
import functools

import jax
import jax.numpy as jnp
from jax import lax
from jax.experimental import pallas as pl
from jax.experimental.pallas import tpu as pltpu
from jax.sharding import PartitionSpec as P

AXES = ("layer", "row", "col")
BF = jnp.bfloat16
F32 = jnp.float32


USES = (
    ((1, 0), (1, 1), (0, 1), (0, 0)),
    ((0, 0), (1, 0), (1, 1), (0, 1)),
    ((1, 1), (0, 1), (0, 0), (1, 0)),
    ((0, 1), (0, 0), (1, 0), (1, 1)),
)
USE_OF_SLOT = (0, 0, 1, 2, 3, 1, 2)


def sections(slot):
    down, up = (slot + 1) // 2, (6 - slot) // 2
    if slot % 2:
        return down, 0, up, 1
    return up, 1, down, 0


def device(l, zh, core, y, zl):
    return (l * 8 + zh * 2 + core) * 8 + y * 2 + zl


def pairs_of(move, keep):
    found = []
    for l in range(4):
        if l not in keep:
            continue
        for zh in range(4):
            for core in range(2):
                for y in range(4):
                    for zl in range(2):
                        here = device(l, zh, core, y, zl)
                        found.append((here, device(*move(l, zh, core, y, zl))))
    return found


def send(value, move, keep=(0, 1, 2, 3)):
    return lax.ppermute(value, AXES, pairs_of(move, keep))


def order_kernel(pick, ranks, e_left, e_right, o_left, o_right, out, mask, sems):
    lane = lax.broadcasted_iota(jnp.int32, (256, 128), 1) % 64
    line = lax.broadcasted_iota(jnp.int32, (256, 128), 0)
    bound = jnp.zeros((256, 128), jnp.int32)
    for tile in range(16):
        bound = jnp.where(line == tile, ranks[tile], bound)
    direction = pick[1]

    def copies(right, left):
        return (
            pltpu.make_async_copy(right.at[direction], out.at[pl.ds(0, 16)], sems.at[0]),
            pltpu.make_async_copy(left.at[direction], out.at[pl.ds(16, 16)], sems.at[1]),
        )

    @pl.when(pick[0] == 0)
    def _():
        for copy in copies(e_right, e_left):
            copy.start()

    @pl.when(pick[0] != 0)
    def _():
        for copy in copies(o_right, o_left):
            copy.start()

    mask[...] = jnp.where(lane < bound, 1.0, 0.0).astype(BF)
    last = pltpu.make_async_copy(mask, out.at[32], sems.at[2])
    last.start()
    for copy in copies(e_right, e_left):
        copy.wait()
    last.wait()


def ordered(pick, ranks, e_left, e_right, o_left, o_right):
    smem = pl.BlockSpec(memory_space=pltpu.SMEM)
    hbm = pl.BlockSpec(memory_space=pl.ANY)
    return pl.pallas_call(
        order_kernel,
        out_shape=jax.ShapeDtypeStruct((33, 256, 128), BF),
        in_specs=[smem, smem, hbm, hbm, hbm, hbm],
        out_specs=hbm,
        scratch_shapes=[pltpu.VMEM((256, 128), BF), pltpu.SemaphoreType.DMA((3,))],
        compiler_params=pltpu.CompilerParams(vmem_limit_bytes=4 * 2**20),
        name="order_factors",
    )(pick, ranks, e_left, e_right, o_left, o_right)


PIECES = ((32, 1), (0, 8), (8, 8), (16, 8), (24, 8))


def layer_kernel(
    place, buf, other, source, w_own, w_other, keep, away, factors, xs, stacked, sums, sems
):
    even, core, zl, spot = place[0] == 1, place[1], place[2], place[3]

    def piece(w, index):
        start, size = PIECES[index]
        whole = (w_own, w_other)[w]
        return pltpu.make_async_copy(
            whole.at[pl.ds(start, size)], factors.at[w, pl.ds(start, size)], sems.at[w, index]
        )

    for w in range(2):
        for index in range(5):
            piece(w, index).start()

    for w in range(2):
        half = zl if w == 0 else 1 - zl
        for chunk in range(8):
            from_other = jnp.logical_and(even, core != chunk % 2)
            index = jnp.where(even, chunk // 2 * 2 + half, chunk)
            flag = jnp.full((128, 128), from_other.astype(jnp.int32)) != 0
            value = jnp.where(flag, other[index].astype(F32), buf[index].astype(F32)).astype(BF)
            xs[w, chunk // 2, :, chunk % 2 * 128 : chunk % 2 * 128 + 128] = value

    lane = lax.broadcasted_iota(jnp.int32, (1, 128), 1)
    sign = jnp.where(lane < 64, 1.0, -1.0)
    for w in range(2):
        piece(w, 0).wait()
        masks = factors[w, 32, 0:16, :].astype(F32)
        for a_pair in range(2):
            piece(w, 1 + a_pair).wait()
            for c in range(4):
                tiles = (a_pair * 8 + c, a_pair * 8 + 4 + c)
                right = jnp.concatenate([factors[w, tile] for tile in tiles], axis=1)
                product = jnp.dot(xs[w, c], right, preferred_element_type=F32)
                for side in range(2):
                    part = product[:, side * 128 : side * 128 + 128]
                    turned = pltpu.roll(part, 64, 1)
                    turned = jnp.concatenate([-turned[64:], turned[:64]], axis=0)
                    mask = masks[tiles[side] : tiles[side] + 1]
                    value = (part * sign + turned) * mask
                    stacked[w, a_pair * 2 + side, :, c * 128 : c * 128 + 128] = value.astype(BF)
        for a in range(4):
            if a % 2 == 0:
                piece(w, 3 + a // 2).wait()
            total = None
            for c_pair in range(2):
                left = jnp.concatenate(
                    [factors[w, 16 + a * 4 + c_pair * 2 + side] for side in range(2)], axis=1
                )
                term = lax.dot_general(
                    stacked[w, a, :, c_pair * 256 : c_pair * 256 + 256],
                    left,
                    (((1,), (1,)), ((), ())),
                    preferred_element_type=F32,
                )
                total = term if total is None else total + term
            sums[w, a * 2] = total[:, :128]
            sums[w, a * 2 + 1] = total[:, 128:]

    @pl.when(even)
    def _():
        for chunk in range(8):
            keep[chunk] = sums[0, chunk] + sums[1, chunk]
            away[chunk] = jnp.zeros((128, 128), BF)

    @pl.when(jnp.logical_not(even))
    def _():
        for chunk in range(8):
            w = jnp.where(zl == chunk % 2, 0, 1)
            keep[chunk] = sums[w, chunk // 2 * 2 + core]
            away[chunk] = sums[w, chunk // 2 * 2 + 1 - core].astype(BF)

    for side in range(2):
        keep[spot * 2 + side] = keep[spot * 2 + side] + source[side]


def layer(place, buf, other, source, w_own, w_other):
    vmem = pl.BlockSpec(memory_space=pltpu.VMEM)
    hbm = pl.BlockSpec(memory_space=pl.ANY)
    return pl.pallas_call(
        layer_kernel,
        out_shape=(
            jax.ShapeDtypeStruct((8, 128, 128), F32),
            jax.ShapeDtypeStruct((8, 128, 128), BF),
        ),
        in_specs=[pl.BlockSpec(memory_space=pltpu.SMEM), vmem, vmem, vmem, hbm, hbm],
        out_specs=(vmem, vmem),
        scratch_shapes=[
            pltpu.VMEM((2, 33, 256, 128), BF),
            pltpu.VMEM((2, 4, 128, 256), BF),
            pltpu.VMEM((2, 4, 128, 512), BF),
            pltpu.VMEM((2, 8, 128, 128), F32),
            pltpu.SemaphoreType.DMA((2, 5)),
        ],
        compiler_params=pltpu.CompilerParams(vmem_limit_bytes=20 * 2**20),
        cost_estimate=pl.CostEstimate(
            flops=32 * 2 * 128 * 256 * 256, bytes_accessed=6 * 2**20, transcendentals=0
        ),
        name="layer_product",
    )(place, buf, other, source, w_own, w_other)


def on_device(
    even_left, even_right, odd_left, odd_right, even_ranks, odd_ranks, even_sources, odd_sources
):
    section = lax.axis_index("layer")
    row, col = lax.axis_index("row"), lax.axis_index("col")
    zh, core, y, zl = row // 2, row % 2, col // 2, col % 2

    table = jnp.array(USES, jnp.int32)[section]
    flat = [f.reshape(2, 16, 256, 128) for f in (even_left, even_right, odd_left, odd_right)]
    ranks = jnp.stack([even_ranks.reshape(2, 16), odd_ranks.reshape(2, 16)])
    own = []
    for use in range(4):
        pick = table[use]
        own.append(ordered(pick, ranks[pick[0], pick[1]], *flat))
    swap_zl = lambda l, zh, core, y, zl: (l, zh, core, y, 1 - zl)
    swap_core = lambda l, zh, core, y, zl: (l, zh, 1 - core, y, zl)

    sources = jnp.concatenate([even_sources[:, 0], odd_sources[:, 0]])
    sources = jnp.swapaxes(sources, 2, 3)
    mine = lax.dynamic_index_in_dim(sources, zl, 1, keepdims=False)
    theirs = send(lax.dynamic_index_in_dim(sources, 1 - zl, 1, keepdims=False), swap_zl)
    first = zl == 0
    pair = jnp.stack([jnp.where(first, mine, theirs), jnp.where(first, theirs, mine)], axis=1)
    partner = [send(factors, swap_zl) for factors in own]

    def roles(slot):
        even_sec, even_dir, odd_sec, odd_dir = sections(slot)
        even = section == even_sec
        spot = jnp.where(even, y, zh)
        which = jnp.where(even, even_dir, 2 + odd_dir)
        return even, spot, lax.dynamic_index_in_dim(pair, which, 0, keepdims=False)

    def total(value, slot):
        even_sec, _, odd_sec, _ = sections(slot)
        both = (even_sec, odd_sec)

        def flip(bits):
            def move(l, zh, core, y, zl):
                if l == even_sec:
                    return (l, zh, core, y ^ bits, zl)
                return (l, zh ^ bits, core, y, zl)

            return move

        low, high = value[:4], value[4:]
        low_in = send(low.astype(BF), flip(1), both)
        high_in = send(high.astype(BF), flip(3), both)
        low, high = low + low_in.astype(F32), high + high_in.astype(F32)
        low_in = send(low.astype(BF), flip(3), both)
        high_in = send(high.astype(BF), flip(1), both)
        return jnp.concatenate([low + low_in.astype(F32), high + high_in.astype(F32)])

    def next_input(value, slot):
        buf = value.astype(BF)
        even_sec, even_dir, odd_sec, odd_dir = sections(slot)
        if slot in (0, 2, 4):
            step = {even_sec: 1 - 2 * even_dir, odd_sec: 1 - 2 * odd_dir}
            buf = send(
                buf, lambda l, zh, core, y, zl: (l + step[l], zh, core, y, zl), (even_sec, odd_sec)
            )
        other = send(buf, swap_core, (sections(slot + 1)[0],))
        return buf, other

    even, spot, source = roles(-1)
    start = lax.dynamic_update_slice_in_dim(
        jnp.zeros((8, 128, 128), F32), source, spot * 2, 0
    )
    even_sum = jnp.where(section == 0, pair[0], 0.0)
    odd_sum = jnp.where(section == 3, pair[3], 0.0)
    buf, other = next_input(total(start, -1), -1)
    for slot in range(7):
        even_sec, _, odd_sec, _ = sections(slot)
        even, spot, source = roles(slot)
        place = jnp.stack([even.astype(jnp.int32), core, zl, spot])
        use = USE_OF_SLOT[slot]
        keep, away = layer(place, buf, other, source, own[use], partner[use])
        keep = keep + send(away, swap_core, (odd_sec,)).astype(F32)
        result = total(keep, slot)
        part = lax.dynamic_slice_in_dim(result, spot * 2, 2, 0)
        even_sum = even_sum + jnp.where(section == even_sec, part, 0.0)
        odd_sum = odd_sum + jnp.where(section == odd_sec, part, 0.0)
        if slot < 6:
            buf, other = next_input(result, slot)

    both = jnp.stack([even_sum, odd_sum])
    mine = lax.dynamic_index_in_dim(both, zl, 1, keepdims=False)
    theirs = send(lax.dynamic_index_in_dim(both, 1 - zl, 1, keepdims=False), swap_zl)
    whole = jnp.stack([jnp.where(first, mine, theirs), jnp.where(first, theirs, mine)], axis=1)
    whole = jnp.swapaxes(whole, 2, 3)
    return whole[0][None], whole[1][None]


def solution(mesh):
    in_specs = (
        P(None, "layer", "row", "col", None, None),
        P(None, "layer", "row", "col", None, None),
        P(None, "layer", "col", "row", None, None),
        P(None, "layer", "col", "row", None, None),
        P(None, "layer", "row", "col"),
        P(None, "layer", "col", "row"),
        P(None, "layer", None, ("row", "col"), None),
        P(None, "layer", None, ("col", "row"), None),
    )
    out_specs = (P("layer", None, ("row", "col"), None), P("layer", None, ("col", "row"), None))
    return jax.shard_map(
        on_device, mesh=mesh, in_specs=in_specs, out_specs=out_specs, check_vma=False
    )
```

```python
import functools

import jax
import jax.numpy as jnp
from jax import lax
from jax.experimental import pallas as pl
from jax.experimental.pallas import tpu as pltpu
from jax.sharding import PartitionSpec as P

AXES = ("layer", "row", "col")
BF = jnp.bfloat16
F32 = jnp.float32


def down_section(slot):
    return (slot + 1) // 2 if slot <= 6 else -1


def up_section(slot):
    return (7 - slot) // 2


def here():
    row, col = lax.axis_index("row"), lax.axis_index("col")
    return lax.axis_index("layer"), row // 2, row % 2, col // 2, col % 2


def send(value, move, sections):
    pairs = []
    for l in sections:
        for zh in range(4):
            for core in range(2):
                target = move(l, zh, core)
                if target is None:
                    continue
                to_l, to_zh, to_core = target
                for col in range(8):
                    pairs.append(
                        (
                            (l * 8 + zh * 2 + core) * 8 + col,
                            (to_l * 8 + to_zh % 4 * 2 + to_core) * 8 + col,
                        )
                    )
    return lax.ppermute(value, AXES, pairs)


PIECES = ((0, 8), (8, 8))


def product_kernel(odd, choose, ranks, *refs):
    if odd:
        trace, right, left, keep, away, rights, lefts, xs, stacked, sems = refs
    else:
        trace, other, right, left, out, rights, lefts, xs, stacked, sems = refs
    section, zh, core, _, _ = here()
    direction = choose if isinstance(choose, int) else (section == choose[0]).astype(jnp.int32)

    def piece(index):
        source, kept = ((right, rights), (left, lefts))[index // 2]
        start, size = PIECES[index % 2]
        return pltpu.make_async_copy(
            source.at[direction, pl.ds(start, size)], kept.at[pl.ds(start, size)], sems.at[index]
        )

    for index in range(4):
        piece(index).start()

    for chunk in range(8):
        lanes = slice(chunk % 2 * 128, chunk % 2 * 128 + 128)
        if odd:
            xs[chunk // 2, :, lanes] = trace[chunk]
        else:
            place = (zh - chunk // 2 + 4) % 4

            @pl.when(core == chunk % 2)
            def _(chunk=chunk, lanes=lanes, place=place):
                xs[chunk // 2, :, lanes] = trace[place]

            @pl.when(core != chunk % 2)
            def _(chunk=chunk, lanes=lanes, place=place):
                xs[chunk // 2, :, lanes] = other[place]

    lane = lax.broadcasted_iota(jnp.int32, (1, 128), 1)
    sign = jnp.where(lane < 64, 1.0, -1.0)
    for a_pair in range(2):
        piece(a_pair).wait()
        for c in range(4):
            tiles = (a_pair * 8 + c, a_pair * 8 + 4 + c)
            joined = jnp.concatenate([rights[tile] for tile in tiles], axis=1)
            product = jnp.dot(xs[c], joined, preferred_element_type=F32)
            for side in range(2):
                part = product[:, side * 128 : side * 128 + 128]
                turned = pltpu.roll(part, 64, 1)
                turned = jnp.concatenate(
                    [-turned[64:128], turned[:64], -turned[192:], turned[128:192]], axis=0
                )
                mask = jnp.where(lane % 64 < ranks[direction, tiles[side]], 1.0, 0.0)
                value = (part * sign + turned) * mask
                stacked[a_pair * 2 + side, :, c * 128 : c * 128 + 128] = value.astype(BF)
    for a in range(4):
        if a % 2 == 0:
            piece(2 + a // 2).wait()
        total = None
        for c_pair in range(2):
            joined = jnp.concatenate(
                [lefts[a * 4 + c_pair * 2 + side] for side in range(2)], axis=1
            )
            term = lax.dot_general(
                stacked[a, :, c_pair * 256 : c_pair * 256 + 256],
                joined,
                (((1,), (1,)), ((), ())),
                preferred_element_type=F32,
            )
            total = term if total is None else total + term
        first, second = total[:, :128], total[:, 128:]
        if odd:
            place = (a - zh + 4) % 4

            @pl.when(core == 0)
            def _(first=first, second=second, place=place):
                keep[place] = first
                away[place] = second.astype(BF)

            @pl.when(core != 0)
            def _(first=first, second=second, place=place):
                keep[place] = second
                away[place] = first.astype(BF)

        else:
            out[a * 2] = first.astype(BF)
            out[a * 2 + 1] = second.astype(BF)


def product(odd, choose, ranks, traces, right, left):
    smem = pl.BlockSpec(memory_space=pltpu.SMEM)
    vmem = pl.BlockSpec(memory_space=pltpu.VMEM)
    hbm = pl.BlockSpec(memory_space=pltpu.HBM)
    if odd:
        shapes = (
            jax.ShapeDtypeStruct((4, 256, 128), F32),
            jax.ShapeDtypeStruct((4, 256, 128), BF),
        )
    else:
        shapes = jax.ShapeDtypeStruct((8, 256, 128), BF)
    return pl.pallas_call(
        functools.partial(product_kernel, odd, choose),
        out_shape=shapes,
        in_specs=[smem] + [vmem] * len(traces) + [hbm, hbm],
        out_specs=(vmem, vmem) if odd else vmem,
        scratch_shapes=[
            pltpu.VMEM((16, 256, 128), BF),
            pltpu.VMEM((16, 256, 128), BF),
            pltpu.VMEM((4, 256, 256), BF),
            pltpu.VMEM((4, 256, 512), BF),
            pltpu.SemaphoreType.DMA((4,)),
        ],
        compiler_params=pltpu.CompilerParams(vmem_limit_bytes=60 * 2**20),
        cost_estimate=pl.CostEstimate(
            flops=16 * 2 * 256**3, bytes_accessed=3 * 2**20, transcendentals=0
        ),
        name="odd_product" if odd else "even_product",
    )(ranks, *traces, right, left)


def on_device(
    even_left, even_right, odd_left, odd_right, even_ranks, odd_ranks, even_sources, odd_sources
):
    section = lax.axis_index("layer")
    even_left, even_right, odd_left, odd_right = (
        factor.reshape(2, 16, 256, 128) for factor in (even_left, even_right, odd_left, odd_right)
    )
    even_ranks, odd_ranks = even_ranks.reshape(2, 16), odd_ranks.reshape(2, 16)
    even_src = jnp.swapaxes(even_sources[:, 0], 2, 3).reshape(2, 256, 128)
    odd_src = jnp.swapaxes(odd_sources[:, 0], 2, 3).reshape(2, 256, 128)

    def odd_terms(traces, slot):
        return product(True, (up_section(slot),), odd_ranks, traces, odd_right, odd_left)

    def even_terms(traces, choose):
        return product(False, choose, even_ranks, traces, even_right, even_left)

    def swap_core(value):
        return send(value, lambda l, zh, core: (l, zh, 1 - core), range(4))

    def row_sum(keep, away):
        summed = keep + swap_core(away).astype(F32)
        total = summed[0]
        for shift in (1, 2, 3):
            part = summed[shift].astype(BF)
            part = send(part, lambda l, zh, core: (l, zh + shift, core), range(4))
            total = total + part.astype(F32)
        return total

    def row_spread(value, moves):
        value = value.astype(BF)
        parts = []
        for shift in range(4):

            def move(l, zh, core):
                if shift == 0 and moves[l] == l:
                    return None
                return (moves[l], zh + shift, core)

            if shift == 0 and all(l == moves[l] for l in moves):
                parts.append(value)
                continue
            part = send(value, move, tuple(moves))
            if shift == 0:
                for l in moves:
                    if moves[l] == l:
                        part = jnp.where(section == l, value, part)
            parts.append(part)
        buf = jnp.stack(parts)
        return buf, swap_core(buf)

    def col_sum(terms):
        terms = lax.all_to_all(terms, "col", 0, 0, tiled=True)
        return jnp.sum(terms.astype(F32), axis=0)

    def col_spread(value):
        value = jnp.broadcast_to(value.astype(BF)[None], (8, 256, 128))
        return lax.all_to_all(value, "col", 0, 0, tiled=True)

    even_sum = jnp.where(section == 0, even_src[0], 0.0)
    odd_sum = jnp.zeros((256, 128), F32)
    trace = col_spread(even_src[0])
    down_traces = None
    for slot in range(8):
        down, up = down_section(slot), up_section(slot)
        if slot % 2 == 0:
            total = row_sum(*odd_terms((trace,), slot))
            if slot == 0:
                total = jnp.where(section == up, odd_src[1], total + odd_src[0])
            else:
                total = total + jnp.where(section == up, odd_src[1], odd_src[0])
            active = jnp.logical_or(section == down, section == up)
            odd_sum = odd_sum + jnp.where(active, total, 0.0)
            if slot == 2:
                traces = row_spread(total, {up: up})
                down_traces = row_spread(total, {down: down + 1})
            elif slot == 6:
                traces = row_spread(total, {up: up})
            else:
                traces = row_spread(total, {down: down + 1, up: up})
            continue
        if slot == 3:
            terms = even_terms(down_traces, 0), even_terms(traces, 1)
            terms = lax.all_to_all(jnp.concatenate(terms, axis=1), "col", 0, 0, tiled=True)
            terms = jnp.sum(terms.astype(F32), axis=0)
            down_total, up_total = terms[:256] + even_src[0], terms[256:] + even_src[1]
            even_sum = even_sum + jnp.where(section == down, down_total + up_total, 0.0)
        else:
            total = col_sum(even_terms(traces, (up,)))
            total = total + jnp.where(section == up, even_src[1], even_src[0])
            active = jnp.logical_or(section == down, section == up)
            even_sum = even_sum + jnp.where(active, total, 0.0)
            down_total = up_total = total
        if slot < 7:
            moved = send(up_total.astype(BF), lambda l, zh, core: (l - 1, zh, core), (up,))
            trace = col_spread(jnp.where(section == up - 1, moved, down_total.astype(BF)))

    even_traces = jnp.swapaxes(even_sum.reshape(2, 128, 128), 1, 2)
    odd_traces = jnp.swapaxes(odd_sum.reshape(2, 128, 128), 1, 2)
    return even_traces[None], odd_traces[None]


def solution(mesh):
    in_specs = (
        P(None, "layer", "row", "col", None, None),
        P(None, "layer", "row", "col", None, None),
        P(None, "layer", "col", "row", None, None),
        P(None, "layer", "col", "row", None, None),
        P(None, "layer", "row", "col"),
        P(None, "layer", "col", "row"),
        P(None, "layer", None, ("row", "col"), None),
        P(None, "layer", None, ("col", "row"), None),
    )
    out_specs = (P("layer", None, ("row", "col"), None), P("layer", None, ("col", "row"), None))
    return jax.shard_map(
        on_device, mesh=mesh, in_specs=in_specs, out_specs=out_specs, check_vma=False
    )
```

```python
import functools

import jax
import jax.numpy as jnp
from jax import lax
from jax.experimental import pallas as pl
from jax.experimental.pallas import tpu as pltpu
from jax.sharding import PartitionSpec as P

AXES = ("layer", "row", "col")
BF = jnp.bfloat16
F32 = jnp.float32


def down_section(slot):
    return (slot + 1) // 2 if slot <= 6 else -1


def up_section(slot):
    return (7 - slot) // 2


def here():
    row, col = lax.axis_index("row"), lax.axis_index("col")
    return lax.axis_index("layer"), row // 2, row % 2, col // 2, col % 2


def send(value, move, sections):
    pairs = []
    for l in sections:
        for zh in range(4):
            for core in range(2):
                target = move(l, zh, core)
                if target is None:
                    continue
                to_l, to_zh, to_core = target
                for col in range(8):
                    pairs.append(
                        (
                            (l * 8 + zh * 2 + core) * 8 + col,
                            (to_l * 8 + to_zh % 4 * 2 + to_core) * 8 + col,
                        )
                    )
    return lax.ppermute(value, AXES, pairs)


def product_kernel(odd, choose, turn, ranks, *refs):
    if odd:
        trace, right, left, keep, away, xs, stacked, lefts, rights, sems = refs
    else:
        trace, other, right, left, out, xs, stacked, lefts, sems = refs
    section, zh, core, _, _ = here()
    direction = choose if isinstance(choose, int) else (section == choose[0]).astype(jnp.int32)

    def piece(index):
        source, kept = ((left, lefts), (right, rights))[index // 2]
        start, size = index % 2 * 8, 8
        return pltpu.make_async_copy(
            source.at[direction, pl.ds(start, size)], kept.at[pl.ds(start, size)], sems.at[index]
        )

    if odd:
        piece(2).start()
        piece(3).start()
    else:
        rights = None
        piece(0).start()
        piece(1).start()

    for chunk in range(8):
        lanes = slice(chunk % 2 * 128, chunk % 2 * 128 + 128)
        if odd:
            xs[chunk // 2, :, lanes] = trace[chunk]
        else:
            place = (zh - chunk // 2 + 4) % 4 if turn else chunk // 2

            @pl.when(core == chunk % 2)
            def _(chunk=chunk, lanes=lanes, place=place):
                xs[chunk // 2, :, lanes] = trace[place]

            @pl.when(core != chunk % 2)
            def _(chunk=chunk, lanes=lanes, place=place):
                xs[chunk // 2, :, lanes] = other[place]

    lane = lax.broadcasted_iota(jnp.int32, (1, 128), 1)
    sign = jnp.where(lane < 64, 1.0, -1.0)
    for a_pair in range(2):
        if odd:
            piece(2 + a_pair).wait()
            piece(a_pair).start()
        for c in range(4):
            tiles = (a_pair * 8 + c, a_pair * 8 + 4 + c)
            joined = jnp.concatenate([rights[tile] if odd else right[direction, tile] for tile in tiles], axis=1)
            product = jnp.dot(xs[c], joined, preferred_element_type=F32)
            for side in range(2):
                part = product[:, side * 128 : side * 128 + 128]
                turned = pltpu.roll(part, 64, 1)
                mask = jnp.where(lane % 64 < ranks[direction, 0, a_pair * 2 + side, c], 1.0, 0.0)
                part, turned = part * (sign * mask), turned * mask
                lanes = slice(c * 128, c * 128 + 128)
                for start in (0, 128):
                    real, imag = slice(start, start + 64), slice(start + 64, start + 128)
                    value = part[real] - turned[imag]
                    stacked[a_pair * 2 + side, real, lanes] = value.astype(BF)
                    value = part[imag] + turned[real]
                    stacked[a_pair * 2 + side, imag, lanes] = value.astype(BF)
    for a in range(4):
        if a % 2 == 0:
            piece(a // 2).wait()
        total = None
        for c_pair in range(2):
            joined = jnp.concatenate(
                [lefts[a * 4 + c_pair * 2 + side] for side in range(2)], axis=1
            )
            term = lax.dot_general(
                stacked[a, :, c_pair * 256 : c_pair * 256 + 256],
                joined,
                (((1,), (1,)), ((), ())),
                preferred_element_type=F32,
            )
            total = term if total is None else total + term
        first, second = total[:, :128], total[:, 128:]
        if odd:
            place = (a - zh + 4) % 4 if turn else a

            @pl.when(core == 0)
            def _(first=first, second=second, place=place):
                keep[place] = first
                away[place] = second.astype(BF)

            @pl.when(core != 0)
            def _(first=first, second=second, place=place):
                keep[place] = second
                away[place] = first.astype(BF)

        else:
            out[a * 2] = first.astype(BF)
            out[a * 2 + 1] = second.astype(BF)


def product(odd, choose, ranks, traces, right, left, turn=True):
    smem = pl.BlockSpec(memory_space=pltpu.SMEM)
    vmem = pl.BlockSpec(memory_space=pltpu.VMEM)
    hbm = pl.BlockSpec(memory_space=pltpu.HBM)
    left = pltpu.with_memory_space_constraint(left, pltpu.HBM)
    if odd:
        right = pltpu.with_memory_space_constraint(right, pltpu.HBM)
        shapes = (
            jax.ShapeDtypeStruct((4, 256, 128), F32),
            jax.ShapeDtypeStruct((4, 256, 128), BF),
        )
    else:
        shapes = jax.ShapeDtypeStruct((8, 256, 128), BF)
    return pl.pallas_call(
        functools.partial(product_kernel, odd, choose, turn),
        out_shape=shapes,
        in_specs=[smem] + [vmem] * len(traces) + [hbm if odd else vmem, hbm],
        out_specs=(vmem, vmem) if odd else vmem,
        scratch_shapes=[
            pltpu.VMEM((4, 256, 256), BF),
            pltpu.VMEM((4, 256, 512), BF),
        ]
        + [pltpu.VMEM((16, 256, 128), BF)] * (2 if odd else 1)
        + [pltpu.SemaphoreType.DMA((4,))],
        compiler_params=pltpu.CompilerParams(vmem_limit_bytes=20 * 2**20),
        cost_estimate=pl.CostEstimate(
            flops=16 * 2 * 256**3, bytes_accessed=3 * 2**20, transcendentals=0
        ),
        name="odd_product" if odd else "even_product",
    )(ranks, *traces, right, left)


def on_device(
    even_left, even_right, odd_left, odd_right, even_ranks, odd_ranks, even_sources, odd_sources
):
    section = lax.axis_index("layer")
    even_left, even_right, odd_left, odd_right = (
        factor.reshape(2, 16, 256, 128) for factor in (even_left, even_right, odd_left, odd_right)
    )
    even_src = jnp.swapaxes(even_sources[:, 0], 2, 3).reshape(2, 256, 128)
    odd_src = jnp.swapaxes(odd_sources[:, 0], 2, 3).reshape(2, 256, 128)

    def odd_terms(traces, slot):
        choose = (up_section(slot),)
        return product(True, choose, odd_ranks, traces, odd_right, odd_left, slot < 6)

    def even_terms(traces, choose, turn=True):
        return product(False, choose, even_ranks, traces, even_right, even_left, turn)

    def swap_core(value):
        return send(value, lambda l, zh, core: (l, zh, 1 - core), range(4))

    def row_sum(keep, away):
        summed = keep + swap_core(away).astype(F32)
        total = summed[0]
        for shift in (1, 2, 3):
            part = summed[shift].astype(BF)
            part = send(part, lambda l, zh, core: (l, zh + shift, core), range(4))
            total = total + part.astype(F32)
        return total

    def row_whole(keep, away, source):
        value = keep + swap_core(away).astype(F32)
        own = zh_mask * source[None]
        value = value + own
        flips = [lambda l, zh, core, bits=bits: (l, zh ^ bits, core) for bits in (1, 3)]
        low, high = value[:2], value[2:]
        for first, second in (flips, flips[::-1]):
            low_in = send(low.astype(BF), first, range(4))
            high_in = send(high.astype(BF), second, range(4))
            low, high = low + low_in.astype(F32), high + high_in.astype(F32)
        value = jnp.concatenate([low, high])
        buf = value.astype(BF)
        return jnp.sum(value * zh_mask, axis=0), (buf, swap_core(buf))

    def row_spread(value, moves):
        value = value.astype(BF)
        parts = []
        for shift in range(4):

            def move(l, zh, core):
                if shift == 0 and moves[l] == l:
                    return None
                return (moves[l], zh + shift, core)

            if shift == 0 and all(l == moves[l] for l in moves):
                parts.append(value)
                continue
            part = send(value, move, tuple(moves))
            if shift == 0:
                for l in moves:
                    if moves[l] == l:
                        part = jnp.where(section == l, value, part)
            parts.append(part)
        buf = jnp.stack(parts)
        return buf, swap_core(buf)

    def col_sum(terms):
        terms = lax.all_to_all(terms, "col", 0, 0, tiled=True)
        return jnp.sum(terms.astype(F32), axis=0)

    def col_spread(value):
        value = jnp.broadcast_to(value.astype(BF)[None], (8, 256, 128))
        return lax.all_to_all(value, "col", 0, 0, tiled=True)

    zh_mask = (lax.iota(jnp.int32, 4) == here()[1]).astype(F32)[:, None, None]
    even_sum = jnp.where(section == 0, even_src[0], 0.0)
    odd_sum = jnp.zeros((256, 128), F32)
    trace = col_spread(even_src[0])
    down_traces = None
    for slot in range(8):
        down, up = down_section(slot), up_section(slot)
        if slot % 2 == 0:
            if slot == 6:
                source = jnp.where(section == up, odd_src[1], odd_src[0])
                total, traces = row_whole(*odd_terms((trace,), slot), source)
                active = jnp.logical_or(section == down, section == up)
                odd_sum = odd_sum + jnp.where(active, total, 0.0)
                continue
            total = row_sum(*odd_terms((trace,), slot))
            if slot == 0:
                total = jnp.where(section == up, odd_src[1], total + odd_src[0])
            else:
                total = total + jnp.where(section == up, odd_src[1], odd_src[0])
            active = jnp.logical_or(section == down, section == up)
            odd_sum = odd_sum + jnp.where(active, total, 0.0)
            if slot == 2:
                traces = row_spread(total, {up: up})
                down_traces = row_spread(total, {down: down + 1})
            else:
                traces = row_spread(total, {down: down + 1, up: up})
            continue
        if slot == 3:
            terms = even_terms(down_traces, 0), even_terms(traces, 1)
            terms = lax.all_to_all(jnp.concatenate(terms, axis=1), "col", 0, 0, tiled=True)
            terms = jnp.sum(terms.astype(F32), axis=0)
            down_total, up_total = terms[:256] + even_src[0], terms[256:] + even_src[1]
            even_sum = even_sum + jnp.where(section == down, down_total + up_total, 0.0)
        else:
            total = col_sum(even_terms(traces, (up,), slot < 7))
            total = total + jnp.where(section == up, even_src[1], even_src[0])
            active = jnp.logical_or(section == down, section == up)
            even_sum = even_sum + jnp.where(active, total, 0.0)
            down_total = up_total = total
        if slot < 7:
            moved = send(up_total.astype(BF), lambda l, zh, core: (l - 1, zh, core), (up,))
            trace = col_spread(jnp.where(section == up - 1, moved, down_total.astype(BF)))

    even_traces = jnp.swapaxes(even_sum.reshape(2, 128, 128), 1, 2)
    odd_traces = jnp.swapaxes(odd_sum.reshape(2, 128, 128), 1, 2)
    return even_traces[None], odd_traces[None]


def solution(mesh):
    in_specs = (
        P(None, "layer", "row", "col", None, None),
        P(None, "layer", "row", "col", None, None),
        P(None, "layer", "col", "row", None, None),
        P(None, "layer", "col", "row", None, None),
        P(None, "layer", "row", "col"),
        P(None, "layer", "col", "row"),
        P(None, "layer", None, ("row", "col"), None),
        P(None, "layer", None, ("col", "row"), None),
    )
    out_specs = (P("layer", None, ("row", "col"), None), P("layer", None, ("col", "row"), None))
    return jax.shard_map(
        on_device, mesh=mesh, in_specs=in_specs, out_specs=out_specs, check_vma=False
    )
```

```python
import functools

import jax
import jax.numpy as jnp
from jax import lax
from jax.experimental import pallas as pl
from jax.experimental.pallas import tpu as pltpu
from jax.sharding import PartitionSpec as P

AXES = ("layer", "row", "col")
BF = jnp.bfloat16
F32 = jnp.float32


def down_section(slot):
    return (slot + 1) // 2 if slot <= 6 else -1


def up_section(slot):
    return (7 - slot) // 2


def here():
    row, col = lax.axis_index("row"), lax.axis_index("col")
    return lax.axis_index("layer"), row // 2, row % 2, col // 2, col % 2


def send(value, move, sections):
    pairs = []
    for l in sections:
        for zh in range(4):
            for core in range(2):
                target = move(l, zh, core)
                if target is None:
                    continue
                to_l, to_zh, to_core = target
                for col in range(8):
                    pairs.append(
                        (
                            (l * 8 + zh * 2 + core) * 8 + col,
                            (to_l * 8 + to_zh % 4 * 2 + to_core) * 8 + col,
                        )
                    )
    return lax.ppermute(value, AXES, pairs)


def product_kernel(odd, choose, ranks, *refs):
    if odd:
        trace, right, left, keep, away, xs, stacked, lefts, rights, sems = refs
    else:
        trace, other, right, left, out, xs, stacked, lefts, sems = refs
    section, _, core, _, _ = here()
    direction = choose if isinstance(choose, int) else (section == choose[0]).astype(jnp.int32)

    def piece(index):
        source, kept = ((left, lefts), (right, rights))[index // 2]
        start, size = index % 2 * 8, 8
        return pltpu.make_async_copy(
            source.at[direction, pl.ds(start, size)], kept.at[pl.ds(start, size)], sems.at[index]
        )

    if odd:
        piece(2).start()
        piece(3).start()
    else:
        rights = None
        piece(0).start()
        piece(1).start()

    for chunk in range(8):
        lanes = slice(chunk % 2 * 128, chunk % 2 * 128 + 128)
        if odd:
            xs[chunk // 2, :, lanes] = trace[chunk]
        else:
            place = chunk // 2

            @pl.when(core == chunk % 2)
            def _(chunk=chunk, lanes=lanes, place=place):
                xs[chunk // 2, :, lanes] = trace[place]

            @pl.when(core != chunk % 2)
            def _(chunk=chunk, lanes=lanes, place=place):
                xs[chunk // 2, :, lanes] = other[place]

    lane = lax.broadcasted_iota(jnp.int32, (1, 128), 1)
    sign = jnp.where(lane < 64, 1.0, -1.0)
    for a_pair in range(2):
        if odd:
            piece(2 + a_pair).wait()
            piece(a_pair).start()
        for c in range(4):
            tiles = (a_pair * 8 + c, a_pair * 8 + 4 + c)
            joined = jnp.concatenate([rights[tile] if odd else right[direction, tile] for tile in tiles], axis=1)
            product = jnp.dot(xs[c], joined, preferred_element_type=F32)
            for side in range(2):
                part = product[:, side * 128 : side * 128 + 128]
                turned = pltpu.roll(part, 64, 1)
                mask = jnp.where(lane % 64 < ranks[direction, 0, a_pair * 2 + side, c], 1.0, 0.0)
                part, turned = part * (sign * mask), turned * mask
                lanes = slice(c * 128, c * 128 + 128)
                for start in (0, 128):
                    real, imag = slice(start, start + 64), slice(start + 64, start + 128)
                    value = part[real] - turned[imag]
                    stacked[a_pair * 2 + side, real, lanes] = value.astype(BF)
                    value = part[imag] + turned[real]
                    stacked[a_pair * 2 + side, imag, lanes] = value.astype(BF)
    for a in range(4):
        if a % 2 == 0:
            piece(a // 2).wait()
        total = None
        for c_pair in range(2):
            joined = jnp.concatenate(
                [lefts[a * 4 + c_pair * 2 + side] for side in range(2)], axis=1
            )
            term = lax.dot_general(
                stacked[a, :, c_pair * 256 : c_pair * 256 + 256],
                joined,
                (((1,), (1,)), ((), ())),
                preferred_element_type=F32,
            )
            total = term if total is None else total + term
        first, second = total[:, :128], total[:, 128:]
        if odd:
            place = a

            @pl.when(core == 0)
            def _(first=first, second=second, place=place):
                keep[place] = first
                away[place] = second.astype(BF)

            @pl.when(core != 0)
            def _(first=first, second=second, place=place):
                keep[place] = second
                away[place] = first.astype(BF)

        else:
            out[a * 2] = first.astype(BF)
            out[a * 2 + 1] = second.astype(BF)


def product(odd, choose, ranks, traces, right, left):
    smem = pl.BlockSpec(memory_space=pltpu.SMEM)
    vmem = pl.BlockSpec(memory_space=pltpu.VMEM)
    hbm = pl.BlockSpec(memory_space=pltpu.HBM)
    left = pltpu.with_memory_space_constraint(left, pltpu.HBM)
    if odd:
        right = pltpu.with_memory_space_constraint(right, pltpu.HBM)
        shapes = (
            jax.ShapeDtypeStruct((4, 256, 128), F32),
            jax.ShapeDtypeStruct((4, 256, 128), BF),
        )
    else:
        shapes = jax.ShapeDtypeStruct((8, 256, 128), BF)
    return pl.pallas_call(
        functools.partial(product_kernel, odd, choose),
        out_shape=shapes,
        in_specs=[smem] + [vmem] * len(traces) + [hbm if odd else vmem, hbm],
        out_specs=(vmem, vmem) if odd else vmem,
        scratch_shapes=[
            pltpu.VMEM((4, 256, 256), BF),
            pltpu.VMEM((4, 256, 512), BF),
        ]
        + [pltpu.VMEM((16, 256, 128), BF)] * (2 if odd else 1)
        + [pltpu.SemaphoreType.DMA((4,))],
        compiler_params=pltpu.CompilerParams(vmem_limit_bytes=20 * 2**20),
        cost_estimate=pl.CostEstimate(
            flops=16 * 2 * 256**3, bytes_accessed=3 * 2**20, transcendentals=0
        ),
        name="odd_product" if odd else "even_product",
    )(ranks, *traces, right, left)


def on_device(
    even_left, even_right, odd_left, odd_right, even_ranks, odd_ranks, even_sources, odd_sources
):
    section = lax.axis_index("layer")
    even_left, even_right, odd_left, odd_right = (
        factor.reshape(2, 16, 256, 128) for factor in (even_left, even_right, odd_left, odd_right)
    )
    even_src = jnp.swapaxes(even_sources[:, 0], 2, 3).reshape(2, 256, 128)
    odd_src = jnp.swapaxes(odd_sources[:, 0], 2, 3).reshape(2, 256, 128)

    def odd_terms(traces, slot):
        choose = (up_section(slot),)
        return product(True, choose, odd_ranks, traces, odd_right, odd_left)

    def even_terms(traces, choose):
        return product(False, choose, even_ranks, traces, even_right, even_left)

    def swap_core(value):
        return send(value, lambda l, zh, core: (l, zh, 1 - core), range(4))

    def row_total(keep, away, source, slot):
        down, up = down_section(slot), up_section(slot)
        value = keep + swap_core(away).astype(F32)
        if slot == 0:
            value = jnp.where(section == up, 0.0, value)
        value = value + jnp.where(own_rows, source[None], 0.0)
        low, high = value[:2], value[2:]

        def flip(bits):
            return lambda l, zh, core: (l, zh ^ bits, core)

        low_in = send(low.astype(BF), flip(1), range(4))
        high_in = send(high.astype(BF), flip(3), range(4))
        low, high = low + low_in.astype(F32), high + high_in.astype(F32)
        low_out, high_out = low.astype(BF), high.astype(BF)
        hops = slot < 6

        def outcome(value):
            buf = value.astype(BF)
            return jnp.sum(jnp.where(own_rows, value, 0.0), axis=0), (buf, swap_core(buf))

        def joined(low, high):
            return jnp.concatenate([low, high])

        if not hops:
            low_in = send(low_out, flip(3), range(4)).astype(F32)
            high_in = send(high_out, flip(1), range(4)).astype(F32)
            both = outcome(joined(low + low_in, high + high_in))
            return both, both

        def target(bits, sections):
            def move(l, zh, core):
                return (l + 1 if l == down else l, zh ^ bits, core)

            return lambda part: send(part, move, sections).astype(F32)

        if down + 1 == up:
            up_low = low + target(3, (up,))(low_out)
            up_high = high + target(1, (up,))(high_out)
            down_low = target(3, (down,))(low_out) + target(0, (down,))(low_out)
            down_high = target(1, (down,))(high_out) + target(0, (down,))(high_out)
            return outcome(joined(down_low, down_high)), outcome(joined(up_low, up_high))
        stays = section == up
        low_in = target(3, (down, up))(low_out)
        high_in = target(1, (down, up))(high_out)
        low = low_in + jnp.where(stays, low, target(0, (down,))(low_out))
        high = high_in + jnp.where(stays, high, target(0, (down,))(high_out))
        both = outcome(joined(low, high))
        return both, both

    def col_sum(terms):
        terms = lax.all_to_all(terms, "col", 0, 0, tiled=True)
        return jnp.sum(terms.astype(F32), axis=0)

    def col_spread(value):
        value = jnp.broadcast_to(value.astype(BF)[None], (8, 256, 128))
        return lax.all_to_all(value, "col", 0, 0, tiled=True)

    own_rows = (lax.iota(jnp.int32, 4) == here()[1])[:, None, None]
    even_sum = jnp.where(section == 0, even_src[0], 0.0)
    odd_sum = ahead = jnp.zeros((256, 128), F32)
    trace = col_spread(even_src[0])
    for slot in range(8):
        down, up = down_section(slot), up_section(slot)
        if slot % 2 == 0:
            source = jnp.where(section == up, odd_src[1], odd_src[0])
            keep, away = odd_terms((trace,), slot)
            (down_rows, down_traces), (up_rows, traces) = row_total(keep, away, source, slot)
            odd_sum = odd_sum + jnp.where(section == up, up_rows, 0.0)
            if slot == 6:
                odd_sum = odd_sum + jnp.where(section == down, down_rows, 0.0)
            else:
                ahead = ahead + jnp.where(section == down + 1, down_rows, 0.0)
            continue
        if slot == 3:
            terms = even_terms(down_traces, 0), even_terms(traces, 1)
            terms = lax.all_to_all(jnp.concatenate(terms, axis=1), "col", 0, 0, tiled=True)
            terms = jnp.sum(terms.astype(F32), axis=0)
            down_total, up_total = terms[:256] + even_src[0], terms[256:] + even_src[1]
            even_sum = even_sum + jnp.where(section == down, down_total + up_total, 0.0)
        else:
            total = col_sum(even_terms(traces, (up,)))
            total = total + jnp.where(section == up, even_src[1], even_src[0])
            active = jnp.logical_or(section == down, section == up)
            even_sum = even_sum + jnp.where(active, total, 0.0)
            down_total = up_total = total
        if slot < 7:
            moved = send(up_total.astype(BF), lambda l, zh, core: (l - 1, zh, core), (up,))
            trace = col_spread(jnp.where(section == up - 1, moved, down_total.astype(BF)))

    odd_sum = odd_sum + send(ahead, lambda l, zh, core: (l - 1, zh, core), (1, 2, 3))
    even_traces = jnp.swapaxes(even_sum.reshape(2, 128, 128), 1, 2)
    odd_traces = jnp.swapaxes(odd_sum.reshape(2, 128, 128), 1, 2)
    return even_traces[None], odd_traces[None]


def solution(mesh):
    in_specs = (
        P(None, "layer", "row", "col", None, None),
        P(None, "layer", "row", "col", None, None),
        P(None, "layer", "col", "row", None, None),
        P(None, "layer", "col", "row", None, None),
        P(None, "layer", "row", "col"),
        P(None, "layer", "col", "row"),
        P(None, "layer", None, ("row", "col"), None),
        P(None, "layer", None, ("col", "row"), None),
    )
    out_specs = (P("layer", None, ("row", "col"), None), P("layer", None, ("col", "row"), None))
    return jax.shard_map(
        on_device, mesh=mesh, in_specs=in_specs, out_specs=out_specs, check_vma=False
    )
```

```python
import functools

import jax
import jax.numpy as jnp
from jax import lax
from jax.experimental import pallas as pl
from jax.experimental.pallas import tpu as pltpu
from jax.sharding import PartitionSpec as P

AXES = ("layer", "row", "col")
BF = jnp.bfloat16
F32 = jnp.float32


def down_section(slot):
    return (slot + 1) // 2 if slot <= 6 else -1


def up_section(slot):
    return (7 - slot) // 2


def here():
    row, col = lax.axis_index("row"), lax.axis_index("col")
    return lax.axis_index("layer"), row // 2, row % 2, col // 2, col % 2


def send(value, move, sections):
    pairs = []
    for l in sections:
        for zh in range(4):
            for core in range(2):
                target = move(l, zh, core)
                if target is None:
                    continue
                to_l, to_zh, to_core = target
                for col in range(8):
                    pairs.append(
                        (
                            (l * 8 + zh * 2 + core) * 8 + col,
                            (to_l * 8 + to_zh % 4 * 2 + to_core) * 8 + col,
                        )
                    )
    return lax.ppermute(value, AXES, pairs)


def product_kernel(odd, choose, ranks, *refs):
    if odd:
        trace, right, left, keep, away, xs, stacked, lefts, rights, sems = refs
    else:
        trace, other, right, left, out, xs, stacked, lefts, sems = refs
    section, _, core, _, _ = here()
    direction = choose if isinstance(choose, int) else (section == choose[0]).astype(jnp.int32)

    def piece(index):
        source, kept = ((left, lefts), (right, rights))[index // 4]
        size = 4 if odd else 8
        tiles = pl.ds(index % 4 * size, size)
        return pltpu.make_async_copy(source.at[direction, tiles], kept.at[tiles], sems.at[index])

    if not odd:
        rights = None
    for index in (4, 5, 6, 7, 0, 1, 2, 3) if odd else (0, 1):
        piece(index).start()

    for chunk in range(8):
        lanes = slice(chunk % 2 * 128, chunk % 2 * 128 + 128)
        if odd:
            xs[chunk // 2, :, lanes] = trace[chunk]
        else:
            place = chunk // 2

            @pl.when(core == chunk % 2)
            def _(chunk=chunk, lanes=lanes, place=place):
                xs[chunk // 2, :, lanes] = trace[place]

            @pl.when(core != chunk % 2)
            def _(chunk=chunk, lanes=lanes, place=place):
                xs[chunk // 2, :, lanes] = other[place]

    lane = lax.broadcasted_iota(jnp.int32, (1, 128), 1)
    sign = jnp.where(lane < 64, 1.0, -1.0)
    for a_pair in range(2):
        if odd:
            piece(4 + a_pair * 2).wait()
            piece(5 + a_pair * 2).wait()
        for c in range(4):
            tiles = (a_pair * 8 + c, a_pair * 8 + 4 + c)
            joined = jnp.concatenate([rights[tile] if odd else right[direction, tile] for tile in tiles], axis=1)
            product = jnp.dot(xs[c], joined, preferred_element_type=F32)
            for side in range(2):
                part = product[:, side * 128 : side * 128 + 128]
                turned = pltpu.roll(part, 64, 1)
                mask = jnp.where(lane % 64 < ranks[direction, 0, a_pair * 2 + side, c], 1.0, 0.0)
                part, turned = part * (sign * mask), turned * mask
                lanes = slice(c * 128, c * 128 + 128)
                for start in (0, 128):
                    real, imag = slice(start, start + 64), slice(start + 64, start + 128)
                    value = part[real] - turned[imag]
                    stacked[a_pair * 2 + side, real, lanes] = value.astype(BF)
                    value = part[imag] + turned[real]
                    stacked[a_pair * 2 + side, imag, lanes] = value.astype(BF)
    for a in range(4):
        if odd or a % 2 == 0:
            piece(a if odd else a // 2).wait()
        total = None
        for c_pair in range(2):
            joined = jnp.concatenate(
                [lefts[a * 4 + c_pair * 2 + side] for side in range(2)], axis=1
            )
            term = lax.dot_general(
                stacked[a, :, c_pair * 256 : c_pair * 256 + 256],
                joined,
                (((1,), (1,)), ((), ())),
                preferred_element_type=F32,
            )
            total = term if total is None else total + term
        first, second = total[:, :128], total[:, 128:]
        if odd:
            place = a

            @pl.when(core == 0)
            def _(first=first, second=second, place=place):
                keep[place] = first
                away[place] = second.astype(BF)

            @pl.when(core != 0)
            def _(first=first, second=second, place=place):
                keep[place] = second
                away[place] = first.astype(BF)

        else:
            out[a * 2] = first.astype(BF)
            out[a * 2 + 1] = second.astype(BF)


def product(odd, choose, ranks, traces, right, left):
    smem = pl.BlockSpec(memory_space=pltpu.SMEM)
    vmem = pl.BlockSpec(memory_space=pltpu.VMEM)
    hbm = pl.BlockSpec(memory_space=pltpu.HBM)
    left = pltpu.with_memory_space_constraint(left, pltpu.HBM)
    if odd:
        right = pltpu.with_memory_space_constraint(right, pltpu.HBM)
        shapes = (
            jax.ShapeDtypeStruct((4, 256, 128), F32),
            jax.ShapeDtypeStruct((4, 256, 128), BF),
        )
    else:
        shapes = jax.ShapeDtypeStruct((8, 256, 128), BF)
    return pl.pallas_call(
        functools.partial(product_kernel, odd, choose),
        out_shape=shapes,
        in_specs=[smem] + [vmem] * len(traces) + [hbm if odd else vmem, hbm],
        out_specs=(vmem, vmem) if odd else vmem,
        scratch_shapes=[
            pltpu.VMEM((4, 256, 256), BF),
            pltpu.VMEM((4, 256, 512), BF),
        ]
        + [pltpu.VMEM((16, 256, 128), BF)] * (2 if odd else 1)
        + [pltpu.SemaphoreType.DMA((8,))],
        compiler_params=pltpu.CompilerParams(vmem_limit_bytes=20 * 2**20),
        cost_estimate=pl.CostEstimate(
            flops=16 * 2 * 256**3, bytes_accessed=3 * 2**20, transcendentals=0
        ),
        name="odd_product" if odd else "even_product",
    )(ranks, *traces, right, left)


def on_device(
    even_left, even_right, odd_left, odd_right, even_ranks, odd_ranks, even_sources, odd_sources
):
    section = lax.axis_index("layer")
    even_left, even_right, odd_left, odd_right = (
        factor.reshape(2, 16, 256, 128) for factor in (even_left, even_right, odd_left, odd_right)
    )
    even_src = jnp.swapaxes(even_sources[:, 0], 2, 3).reshape(2, 256, 128)
    odd_src = jnp.swapaxes(odd_sources[:, 0], 2, 3).reshape(2, 256, 128)

    def odd_terms(traces, slot):
        choose = (up_section(slot),)
        return product(True, choose, odd_ranks, traces, odd_right, odd_left)

    def even_terms(traces, choose):
        return product(False, choose, even_ranks, traces, even_right, even_left)

    def swap_core(value):
        return send(value, lambda l, zh, core: (l, zh, 1 - core), range(4))

    def row_total(keep, away, source, slot):
        down, up = down_section(slot), up_section(slot)
        value = keep + swap_core(away).astype(F32)
        if slot == 0:
            value = jnp.where(section == up, 0.0, value)
        value = value + jnp.where(own_rows, source[None], 0.0)
        low, high = value[:2], value[2:]

        def flip(bits):
            return lambda l, zh, core: (l, zh ^ bits, core)

        low_in = send(low.astype(BF), flip(1), range(4))
        high_in = send(high.astype(BF), flip(3), range(4))
        low, high = low + low_in.astype(F32), high + high_in.astype(F32)
        low_out, high_out = low.astype(BF), high.astype(BF)
        hops = slot < 6

        def outcome(value):
            buf = value.astype(BF)
            return jnp.sum(jnp.where(own_rows, value, 0.0), axis=0), (buf, swap_core(buf))

        def joined(low, high):
            return jnp.concatenate([low, high])

        if not hops:
            low_in = send(low_out, flip(3), range(4)).astype(F32)
            high_in = send(high_out, flip(1), range(4)).astype(F32)
            both = outcome(joined(low + low_in, high + high_in))
            return both, both

        def target(bits, sections):
            def move(l, zh, core):
                return (l + 1 if l == down else l, zh ^ bits, core)

            return lambda part: send(part, move, sections).astype(F32)

        if down + 1 == up:
            up_low = low + target(3, (up,))(low_out)
            up_high = high + target(1, (up,))(high_out)
            down_low = target(3, (down,))(low_out) + target(0, (down,))(low_out)
            down_high = target(1, (down,))(high_out) + target(0, (down,))(high_out)
            return outcome(joined(down_low, down_high)), outcome(joined(up_low, up_high))
        stays = section == up
        low_in = target(3, (down, up))(low_out)
        high_in = target(1, (down, up))(high_out)
        low = low_in + jnp.where(stays, low, target(0, (down,))(low_out))
        high = high_in + jnp.where(stays, high, target(0, (down,))(high_out))
        both = outcome(joined(low, high))
        return both, both

    def col_sum(terms):
        terms = lax.all_to_all(terms, "col", 0, 0, tiled=True)
        return jnp.sum(terms.astype(F32), axis=0)

    def col_spread(value):
        value = jnp.broadcast_to(value.astype(BF)[None], (8, 256, 128))
        return lax.all_to_all(value, "col", 0, 0, tiled=True)

    own_rows = (lax.iota(jnp.int32, 4) == here()[1])[:, None, None]
    even_sum = jnp.where(section == 0, even_src[0], 0.0)
    odd_sum = ahead = jnp.zeros((256, 128), F32)
    trace = col_spread(even_src[0])
    for slot in range(8):
        down, up = down_section(slot), up_section(slot)
        if slot % 2 == 0:
            source = jnp.where(section == up, odd_src[1], odd_src[0])
            keep, away = odd_terms((trace,), slot)
            (down_rows, down_traces), (up_rows, traces) = row_total(keep, away, source, slot)
            odd_sum = odd_sum + jnp.where(section == up, up_rows, 0.0)
            if slot == 6:
                odd_sum = odd_sum + jnp.where(section == down, down_rows, 0.0)
            else:
                ahead = ahead + jnp.where(section == down + 1, down_rows, 0.0)
            continue
        if slot == 3:
            terms = even_terms(down_traces, 0), even_terms(traces, 1)
            terms = lax.all_to_all(jnp.concatenate(terms, axis=1), "col", 0, 0, tiled=True)
            terms = jnp.sum(terms.astype(F32), axis=0)
            down_total, up_total = terms[:256] + even_src[0], terms[256:] + even_src[1]
            even_sum = even_sum + jnp.where(section == down, down_total + up_total, 0.0)
        else:
            total = col_sum(even_terms(traces, (up,)))
            total = total + jnp.where(section == up, even_src[1], even_src[0])
            active = jnp.logical_or(section == down, section == up)
            even_sum = even_sum + jnp.where(active, total, 0.0)
            down_total = up_total = total
        if slot < 7:
            moved = send(up_total.astype(BF), lambda l, zh, core: (l - 1, zh, core), (up,))
            trace = col_spread(jnp.where(section == up - 1, moved, down_total.astype(BF)))

    odd_sum = odd_sum + send(ahead, lambda l, zh, core: (l - 1, zh, core), (1, 2, 3))
    even_traces = jnp.swapaxes(even_sum.reshape(2, 128, 128), 1, 2)
    odd_traces = jnp.swapaxes(odd_sum.reshape(2, 128, 128), 1, 2)
    return even_traces[None], odd_traces[None]


def solution(mesh):
    in_specs = (
        P(None, "layer", "row", "col", None, None),
        P(None, "layer", "row", "col", None, None),
        P(None, "layer", "col", "row", None, None),
        P(None, "layer", "col", "row", None, None),
        P(None, "layer", "row", "col"),
        P(None, "layer", "col", "row"),
        P(None, "layer", None, ("row", "col"), None),
        P(None, "layer", None, ("col", "row"), None),
    )
    out_specs = (P("layer", None, ("row", "col"), None), P("layer", None, ("col", "row"), None))
    return jax.shard_map(
        on_device, mesh=mesh, in_specs=in_specs, out_specs=out_specs, check_vma=False
    )
```
